32 devices in a mesh: gx: 8 (over y, x, core), gy: 4 (over z).
Axes of the slice: x: 2, y: 2, z: 4, core: 2. Of those that a mesh axis runs over, the one named last changes fastest.
Arguments:
- sources: bfloat16 [8, 4, 8, 64, 256], P('gx', 'gy'), may hold values from -12 to 12
- geometry: bfloat16 [8, 4, 8, 4, 256], P('gx', 'gy'), may hold values from -0.5 to 0.5, as said below
- near_lists: int32 [8, 4, 8, 24], P('gx', 'gy'), may hold values from -1 to 255, as said below
- far_lists: int32 [8, 4, 4, 16], P('gx', 'gy'), may hold values from 0 to 7, as said below
- bases_in: bfloat16 [8, 4, 4, 32, 8, 256], P('gx', 'gy')
- bases_out: bfloat16 [8, 4, 4, 32, 8, 256], P('gx', 'gy'), may hold values from -0.25 to 0.25
- couplings: float32 [8, 4, 4, 32, 512], P('gx', 'gy')
Outputs:
- potential: float32 [8, 4, 8, 64, 256], P('gx', 'gy')
The draws below stay inside these ranges and needn't reach their ends.
Inputs may be any that keep to these rules, and one draw needn't show every extreme that they name: `near_lists`: for each leaf the first c entries are live, c between 1 and 24 and equal to 24 on some leaves and to 1 on others; the first is the leaf itself, and every live entry names a leaf on a device whose gx and gy indices differ from the leaf's by at most one, in a slot that differs from the leaf's slot by at most one; the other entries are -1. `far_lists`: level 0 entries are below 4, levels 1 and 2 below 8, level 3 below 2. `geometry`: rows 0 to 2 lie in [-0.5, 0.5], row 3 about 0.006 to 0.04.
All inputs are finite; a program needn't handle non-finite values.
Results may differ from the reference program's by a relative error of at most 0.0029.
Values may be sent and summed in bfloat16 or wider, within the bound.
A program may use at most 64 MiB of HBM per device.

```python
import math
import jax
import jax.numpy as jnp
from jax import lax

LEAF = 256
RHS = 64
RANK = 32
LEVELS = 4
NEAR = 24
FAR = 16
LEAF_DEV = 8
ROW_DEVS = 8
COLUMN_DEVS = 4
N_GX = 8
N_GY = 4


def level_groups(shape):
    level = lax.broadcasted_iota(jnp.int32, shape, 2)
    return jnp.where(level == 0, 1, jnp.where(level == 1, 4, jnp.where(level == 2, COLUMN_DEVS, 4 * COLUMN_DEVS))).astype(jnp.float32)


def draw_geometry(key, part):
    keys = jax.random.split(key, 5)
    shape = (ROW_DEVS, COLUMN_DEVS, LEAF_DEV, 3, LEAF)
    face_pick = 3.0 * jax.random.uniform(keys[0], (ROW_DEVS, COLUMN_DEVS, LEAF_DEV, 1, LEAF), jnp.float32)
    component = lax.broadcasted_iota(jnp.int32, shape, 3).astype(jnp.float32)
    on_face = (face_pick >= component) & (face_pick < component + 1.0)
    side = jnp.where(jax.random.uniform(keys[1], shape, jnp.float32) < 0.5, -1.0, 1.0)
    depth_draw = jax.random.uniform(keys[2], shape, jnp.float32)
    tangent_draw = jax.random.uniform(keys[3], shape, jnp.float32, -1.0, 1.0)
    depth = 0.5 - 0.03 * depth_draw
    tangent = 0.5 * jnp.sign(tangent_draw) * jnp.sqrt(jnp.abs(tangent_draw))
    offsets = jnp.where(on_face, side * depth, tangent)
    areas = jnp.exp(jax.random.uniform(keys[4], (ROW_DEVS, COLUMN_DEVS, LEAF_DEV, 1, LEAF), jnp.float32, math.log(0.006), math.log(0.04)))
    return jnp.concatenate([offsets, areas], axis=3).astype(jnp.bfloat16)


def draw_near_lists(key, part):
    keys = jax.random.split(key, 5)
    shape = (ROW_DEVS, COLUMN_DEVS, LEAF_DEV, NEAR)
    row_pos = lax.broadcasted_iota(jnp.int32, shape, 0)
    col_pos = lax.broadcasted_iota(jnp.int32, shape, 1)
    leaf_pos = lax.broadcasted_iota(jnp.int32, shape, 2)
    slot_pos = lax.broadcasted_iota(jnp.int32, shape, 3)
    base = jax.random.randint(keys[0], (ROW_DEVS, COLUMN_DEVS, 1, 1), max(1, NEAR // 4), NEAR + 1)
    count = base - jax.random.randint(keys[1], (ROW_DEVS, COLUMN_DEVS, LEAF_DEV, 1), 0, base // 2 + 1)
    flat = row_pos * COLUMN_DEVS + col_pos
    count = jnp.where((flat % 5 == 0) & (leaf_pos == 0), NEAR, count)
    count = jnp.where((flat % 5 == 1) & (leaf_pos == 0), 1, count)
    src_row = jnp.clip(row_pos + jax.random.randint(keys[2], shape, -1, 2), 0, ROW_DEVS - 1)
    src_col = jnp.clip(col_pos + jax.random.randint(keys[3], shape, -1, 2), 0, COLUMN_DEVS - 1)
    src_leaf = jnp.clip(leaf_pos + jax.random.randint(keys[4], shape, -1, 2), 0, LEAF_DEV - 1)
    leaf_ids = (src_row * COLUMN_DEVS + src_col) * LEAF_DEV + src_leaf
    itself = flat * LEAF_DEV + leaf_pos
    leaf_ids = jnp.where(slot_pos == 0, itself, leaf_ids)
    return jnp.where(slot_pos < count, leaf_ids, -1).astype(jnp.int32)


def draw_far_lists(key, part):
    shape = (ROW_DEVS, COLUMN_DEVS, LEVELS, FAR)
    row_pos = lax.broadcasted_iota(jnp.int32, shape, 0)
    col_pos = lax.broadcasted_iota(jnp.int32, shape, 1)
    level = lax.broadcasted_iota(jnp.int32, shape, 2)
    slot_pos = lax.broadcasted_iota(jnp.int32, shape, 3)
    limit = jnp.where(level == 0, COLUMN_DEVS, jnp.where(level == 3, ROW_DEVS // 4, ROW_DEVS))
    cluster = jax.random.randint(key, shape, 0, limit)
    flat = row_pos * COLUMN_DEVS + col_pos
    return jnp.where(slot_pos == FAR - 1, flat % limit, cluster).astype(jnp.int32)


def draw_bases_in(key, part):
    shape = (ROW_DEVS, COLUMN_DEVS, LEVELS, RANK, LEAF_DEV, LEAF)
    scale = 0.5 * (level_groups(shape) * LEAF_DEV * LEAF) ** (-0.5)
    values = jax.random.normal(key, shape, jnp.float32)
    return (values * scale).astype(jnp.bfloat16)


def draw_couplings(key, part):
    shape = (ROW_DEVS, COLUMN_DEVS, LEVELS, RANK, FAR * RANK)
    scale = (level_groups(shape) * FAR * RANK) ** (-0.5)
    values = jax.random.normal(key, shape, jnp.float32)
    return values * scale


def block_scale(rng, shape, pieces, low, largest):
    def one(axis_at, shards_of):
        heights = jax.random.uniform(jax.random.fold_in(jax.random.fold_in(rng, 6), axis_at), (shards_of,), jnp.float32, low / len(pieces), largest / len(pieces))
        return jnp.repeat(jnp.exp(heights), shape[axis_at] // shards_of).reshape((-1,) + (1,) * (len(shape) - axis_at - 1))

    level = one(*pieces[0])
    for cut in pieces[1:]:
        level = level * one(*cut)
    return level


def bell_draw(own_key, extent, spread, most, cuts=(), kind=jnp.bfloat16):
    entries = jax.random.normal(own_key, extent, jnp.float32) * spread
    if len(cuts) > 0:
        entries = block_scale(own_key, extent, cuts, -0.22, 0.18) * entries
    return jnp.clip(entries, min=-most, max=most).astype(kind)


def setup_inputs(seed: int = 0) -> dict:
    seeds = jax.random.split(jax.random.key(seed), 8)
    return {
        "sources": bell_draw(seeds[0], (ROW_DEVS, COLUMN_DEVS, LEAF_DEV, RHS, LEAF), 2.0, 12.0, ((0, 8), (1, 4))),
        "geometry": draw_geometry(jax.random.fold_in(seeds[7], 71), 0),
        "near_lists": draw_near_lists(jax.random.fold_in(seeds[7], 71), 0),
        "far_lists": draw_far_lists(jax.random.fold_in(seeds[7], 71), 0),
        "bases_in": draw_bases_in(jax.random.fold_in(seeds[7], 71), 0),
        "bases_out": bell_draw(seeds[5], (ROW_DEVS, COLUMN_DEVS, LEVELS, RANK, LEAF_DEV, LEAF), (16 * RANK) ** -0.5, 0.25, ((0, 8), (1, 4))),
        "couplings": draw_couplings(jax.random.fold_in(seeds[7], 71), 0),
    }


FOUR_PI = 4.0 * math.pi

def leaf_centers(leaf_ids):
    device = leaf_ids // LEAF_DEV
    return jnp.stack([device // N_GY, device % N_GY, leaf_ids % LEAF_DEV], axis=-1).astype(jnp.float32)

def near_block(target_geo, target_center, source_geo, source_center, source_vals, weight):
    target_pos = target_geo[:, :3, :].astype(jnp.float32) + target_center[:, :, None]
    source_pos = source_geo[:, :3, :].astype(jnp.float32) + source_center[:, :, None]
    squared = jnp.zeros((target_pos.shape[0], target_pos.shape[2], source_pos.shape[2]), jnp.float32)
    for component in range(3):
        offset = target_pos[:, component, :, None] - source_pos[:, component, None, :]
        squared = squared + offset * offset
    panel_area = source_geo[:, 3, :].astype(jnp.float32)[:, None, :]
    kernel = (weight[:, None, None] * panel_area / (FOUR_PI * jnp.sqrt(squared + panel_area))).astype(jnp.bfloat16)
    kernel = lax.optimization_barrier(kernel)
    return jnp.einsum('lij,lrj->lri', kernel.astype(jnp.float32), source_vals.astype(jnp.float32))

def reference(sources, geometry, near_lists, far_lists, bases_in, bases_out, couplings):
    devices = N_GX * N_GY
    flat_src = sources.reshape(devices * LEAF_DEV, RHS, LEAF)
    flat_geo = geometry.reshape(devices * LEAF_DEV, 4, LEAF)
    lists = near_lists.reshape(devices, LEAF_DEV, NEAR)

    def one_device(packed):
        device, table = packed
        own = device * LEAF_DEV + jnp.arange(LEAF_DEV, dtype=jnp.int32)
        target_geo = flat_geo[own]
        target_center = leaf_centers(own)
        total = jnp.zeros((LEAF_DEV, RHS, LEAF), jnp.float32)
        for slot in range(NEAR):
            leaf_ids = table[:, slot]
            weight = (leaf_ids >= 0).astype(jnp.float32)
            safe = jnp.maximum(leaf_ids, 0).astype(jnp.int32)
            total = total + near_block(target_geo, target_center, flat_geo[safe], leaf_centers(safe), flat_src[safe], weight)
        return total
    near_field = lax.map(one_device, (jnp.arange(devices, dtype=jnp.int32), lists)).reshape(sources.shape)
    projection = jnp.einsum('xyaqlp,xylrp->xyaqr', bases_in.astype(jnp.float32), sources.astype(jnp.float32))
    level_zero = projection[:, :, 0]
    level_one = projection[:, :, 1].reshape(N_GX, N_GY // 4, 4, RANK, RHS).sum(axis=2)
    level_two = projection[:, :, 2].sum(axis=1)
    level_three = projection[:, :, 3].sum(axis=1).reshape(N_GX // 4, 4, RANK, RHS).sum(axis=1)
    row_index = jnp.arange(N_GX, dtype=jnp.int32)[:, None, None]
    quarter_index = (jnp.arange(N_GY, dtype=jnp.int32) // 4)[None, :, None]
    picked_zero = level_zero[row_index, far_lists[:, :, 0]]
    picked_one = level_one[far_lists[:, :, 1], quarter_index]
    picked_two = level_two[far_lists[:, :, 2]]
    picked_three = level_three[far_lists[:, :, 3]]
    gathered = jnp.stack([picked_zero, picked_one, picked_two, picked_three], axis=2)
    gathered = gathered.reshape(N_GX, N_GY, 4, FAR * RANK, RHS)
    interaction = jnp.einsum('xyaqk,xyakr->xyaqr', couplings, gathered, precision=lax.Precision.HIGHEST)
    summed_zero = interaction[:, :, 0]
    summed_one = jnp.repeat(interaction[:, :, 1].reshape(N_GX, N_GY // 4, 4, RANK, RHS).sum(axis=2), 4, axis=1)
    summed_two = jnp.broadcast_to(interaction[:, :, 2].sum(axis=1, keepdims=True), summed_zero.shape)
    coarse_total = interaction[:, :, 3].sum(axis=1).reshape(N_GX // 4, 4, RANK, RHS).sum(axis=1)
    summed_three = jnp.broadcast_to(jnp.repeat(coarse_total, 4, axis=0)[:, None], summed_zero.shape)
    target_sum = jnp.stack([summed_zero, summed_one, summed_two, summed_three], axis=2).astype(jnp.bfloat16)
    target_sum = lax.optimization_barrier(target_sum)
    far_field = jnp.einsum('xyaqr,xyaqlp->xylrp', target_sum.astype(jnp.float32), bases_out.astype(jnp.float32))
    return near_field + far_field
```

```python
import functools
import math

import jax
import jax.numpy as jnp
from jax import lax
from jax.experimental import pallas as pl
from jax.experimental.pallas import tpu as pltpu
from jax.sharding import PartitionSpec as P

FOUR_PI = 4.0 * math.pi
MESH = pl.DeviceIdType.MESH
UNROLL = 2


def exchange_kernel(
    n_gx, n_gy, packed, proj, coup, far, halo, target,
    col_buf, row_src, row_buf, tab3, gath, int_src, int_buf, c3_src, c3_buf,
    halo_s, halo_r, p1_s, p1_r, p2_s, p2_r, p3_s, p3_r, p4_s, p4_r,
):
    x = lax.axis_index("gx")
    y = lax.axis_index("gy")
    barrier = pltpu.get_barrier_semaphore()

    def inside(dx, dy):
        tests = []
        if dx == -1:
            tests.append(x > 0)
        if dx == 1:
            tests.append(x < n_gx - 1)
        if dy == -1:
            tests.append(y > 0)
        if dy == 1:
            tests.append(y < n_gy - 1)
        return functools.reduce(jnp.logical_and, tests)

    offsets = [(dx, dy) for dx in (-1, 0, 1) for dy in (-1, 0, 1) if (dx, dy) != (0, 0)]
    diagonal = [o for o in offsets if o[0] * o[1] != 0]
    count = jnp.int32(n_gx - 1 + n_gy - 1)
    for k in range(1, n_gx):
        pl.semaphore_signal(
            barrier, inc=1, device_id=(lax.rem(x + k, n_gx), y), device_id_type=MESH
        )
    for k in range(1, n_gy):
        pl.semaphore_signal(
            barrier, inc=1, device_id=(x, lax.rem(y + k, n_gy)), device_id_type=MESH
        )
    for dx, dy in diagonal:
        there = inside(dx, dy)
        count = count + there.astype(jnp.int32)

        @pl.when(there)
        def _():
            pl.semaphore_signal(barrier, inc=1, device_id=(x + dx, y + dy), device_id_type=MESH)

    pl.semaphore_wait(barrier, count)

    def remote(src, dst, send, recv, where):
        return pltpu.make_async_remote_copy(
            src_ref=src, dst_ref=dst, send_sem=send, recv_sem=recv,
            device_id=where, device_id_type=MESH,
        )

    def column(src, buf, send, recv):
        for k in range(1, n_gy):
            to = lax.rem(y + k, n_gy)
            remote(src, buf.at[y], send.at[k], recv.at[y], (x, to)).start()
        buf[y] = src[...]

    def column_wait(src, buf, send, recv):
        for k in range(1, n_gy):
            peer = lax.rem(y + k, n_gy)
            remote(src, buf.at[peer], send.at[k], recv.at[peer], (x, peer)).wait_recv()

    column(proj, col_buf, p1_s, p1_r)

    def halo_copy(dx, dy):
        mine = (dx + 1) * 3 + dy + 1
        return remote(
            packed, halo.at[8 - mine], halo_s.at[mine], halo_r.at[8 - mine], (x + dx, y + dy)
        )

    def halo_start(dx, dy):
        @pl.when(inside(dx, dy))
        def _():
            halo_copy(dx, dy).start()

    for dx, dy in offsets:
        halo_start(dx, dy)
    halo[4] = packed[...]

    column_wait(proj, col_buf, p1_s, p1_r)
    quarter = 4 * (y // 4)
    row_src[0:32, :] = sum(col_buf[quarter + g, 32:64, :] for g in range(4))
    row_src[32:96, :] = sum(col_buf[g, 64:128, :] for g in range(n_gy))
    for k in range(1, n_gx):
        to = lax.rem(x + k, n_gx)
        remote(row_src, row_buf.at[x], p2_s.at[k], p2_r.at[x], (to, y)).start()
    row_buf[x] = row_src[...]
    for m in range(16):
        gath[pl.ds(m * 32, 32), :] = col_buf[far[0, m], 0:32, :]
    first = jnp.dot(
        coup[0], gath[...], preferred_element_type=jnp.float32, precision=lax.Precision.HIGHEST
    )
    target[0:32, :] = first.astype(jnp.bfloat16)
    for k in range(1, n_gx):
        peer = lax.rem(x + k, n_gx)
        remote(row_src, row_buf.at[peer], p2_s.at[k], p2_r.at[peer], (peer, y)).wait_recv()
    for c in range(n_gx // 4):
        tab3[c] = sum(row_buf[4 * c + g, 64:96, :] for g in range(4))
    for level in (1, 2, 3):
        for m in range(16):
            s = far[level, m]
            if level == 3:
                gath[pl.ds(m * 32, 32), :] = tab3[s]
            else:
                gath[pl.ds(m * 32, 32), :] = row_buf[s, (level - 1) * 32 : level * 32, :]
        int_src[(level - 1) * 32 : level * 32, :] = jnp.dot(
            coup[level], gath[...], preferred_element_type=jnp.float32,
            precision=lax.Precision.HIGHEST,
        )
    column(int_src, int_buf, p3_s, p3_r)
    column_wait(int_src, int_buf, p3_s, p3_r)
    c3_src[...] = sum(int_buf[g, 64:96, :] for g in range(n_gy))
    base = 4 * (x // 4)
    spot = lax.rem(x, 4)
    for k in range(1, 4):
        to = base + lax.rem(spot + k, 4)
        remote(c3_src, c3_buf.at[spot], p4_s.at[k], p4_r.at[spot], (to, y)).start()
    c3_buf[spot] = c3_src[...]
    target[32:64, :] = sum(int_buf[quarter + g, 0:32, :] for g in range(4)).astype(jnp.bfloat16)
    target[64:96, :] = sum(int_buf[g, 32:64, :] for g in range(n_gy)).astype(jnp.bfloat16)
    for k in range(1, 4):
        peer = lax.rem(spot + k, 4)
        remote(c3_src, c3_buf.at[peer], p4_s.at[k], p4_r.at[peer], (base + peer, y)).wait_recv()
    target[96:128, :] = sum(c3_buf[g] for g in range(4)).astype(jnp.bfloat16)

    for dx, dy in offsets:

        @pl.when(inside(dx, dy))
        def _():
            mine = (dx + 1) * 3 + dy + 1
            remote(
                packed, halo.at[mine], halo_s.at[mine], halo_r.at[mine], (x + dx, y + dy)
            ).wait()

    for k in range(1, n_gy):
        to = lax.rem(y + k, n_gy)
        remote(proj, col_buf.at[y], p1_s.at[k], p1_r.at[y], (x, to)).wait_send()
        remote(int_src, int_buf.at[y], p3_s.at[k], p3_r.at[y], (x, to)).wait_send()
    for k in range(1, n_gx):
        to = lax.rem(x + k, n_gx)
        remote(row_src, row_buf.at[x], p2_s.at[k], p2_r.at[x], (to, y)).wait_send()
    for k in range(1, 4):
        to = base + lax.rem(spot + k, 4)
        remote(c3_src, c3_buf.at[spot], p4_s.at[k], p4_r.at[spot], (to, y)).wait_send()


def exchange(packed, proj, coup, far, n_gx, n_gy):
    rows, panels = packed.shape
    rhs = proj.shape[1]
    vmem = pl.BlockSpec(memory_space=pltpu.VMEM)
    f32 = jnp.float32
    sems = pltpu.SemaphoreType.DMA
    return pl.pallas_call(
        functools.partial(exchange_kernel, n_gx, n_gy),
        out_shape=(
            jax.ShapeDtypeStruct((9, rows, panels), jnp.bfloat16),
            jax.ShapeDtypeStruct((128, rhs), jnp.bfloat16),
        ),
        in_specs=[vmem, vmem, vmem, pl.BlockSpec(memory_space=pltpu.SMEM)],
        out_specs=(vmem, vmem),
        scratch_shapes=[
            pltpu.VMEM((n_gy, 128, rhs), f32),
            pltpu.VMEM((96, rhs), f32),
            pltpu.VMEM((n_gx, 96, rhs), f32),
            pltpu.VMEM((n_gx // 4, 32, rhs), f32),
            pltpu.VMEM((512, rhs), f32),
            pltpu.VMEM((96, rhs), f32),
            pltpu.VMEM((n_gy, 96, rhs), f32),
            pltpu.VMEM((32, rhs), f32),
            pltpu.VMEM((4, 32, rhs), f32),
            sems((9,)), sems((9,)),
            sems((n_gy,)), sems((n_gy,)),
            sems((n_gx,)), sems((n_gx,)),
            sems((n_gy,)), sems((n_gy,)),
            sems((4,)), sems((4,)),
        ],
        compiler_params=pltpu.CompilerParams(
            collective_id=0, has_side_effects=True, vmem_limit_bytes=32 * 1024 * 1024
        ),
    )(packed, proj, coup, far)


def near_kernel(slots, leaf_dev, index, shift, count, live, halo, tfeat, out, sfeat, scale):
    leaf = pl.program_id(0)
    rhs = out.shape[1]

    @pl.when(leaf == 0)
    def _():
        def source_features(place, carry):
            def row(c):
                wide = halo[place, pl.ds(leaf_dev * rhs, 4 * leaf_dev), :].astype(jnp.float32)
                return wide[c * leaf_dev : (c + 1) * leaf_dev]

            sx, sy, sz, area = row(0), row(1), row(2), row(3)
            dx = (place // 3 - 1).astype(jnp.float32)
            dy = (lax.rem(place, 3) - 1).astype(jnp.float32)
            q = (sx + dx) * (sx + dx) + (sy + dy) * (sy + dy) + sz * sz + area
            high = q.astype(jnp.bfloat16).astype(jnp.float32)
            mid = (q - high).astype(jnp.bfloat16).astype(jnp.float32)
            one, zero = jnp.ones_like(q), jnp.zeros_like(q)
            rows = [sx, sy, sz, dx + zero, dy + zero, sz, one, one, one]
            rows += [high, mid, q - high - mid] + [zero] * 4
            own = pl.ds(pl.multiple_of(place * leaf_dev, leaf_dev), leaf_dev)
            for k, value in enumerate(rows):
                sfeat[own, k, :] = value
            scale[own, :] = area * (1.0 / FOUR_PI)
            return carry

        lax.fori_loop(0, 9, source_features, 0)

    out[0] = jnp.zeros(out.shape[1:], jnp.float32)

    def step(pair, carry):
        total = None
        for u in range(UNROLL):
            at = leaf * slots + pair * UNROLL + u
            n = index[at]
            squared = lax.dot_general(
                tfeat[0, shift[at]], sfeat[n].astype(jnp.bfloat16), (((0,), (0,)), ((), ())),
                preferred_element_type=jnp.float32,
            )
            weight = scale[pl.ds(n, 1), :] * live[at].astype(jnp.float32)
            kernel = (lax.rsqrt(squared) * weight).astype(jnp.bfloat16)
            src = halo[n // 8, pl.ds(pl.multiple_of(lax.rem(n, 8) * rhs, rhs), rhs), :]
            term = lax.dot_general(
                src, kernel, (((1,), (1,)), ((), ())), preferred_element_type=jnp.float32
            )
            total = term if total is None else total + term
        out[0] += total
        return carry

    lax.fori_loop(0, (count[leaf] + UNROLL - 1) // UNROLL, step, 0)


def pieces(v):
    high = lax.reduce_precision(v, 8, 7)
    rest = v - high
    mid = lax.reduce_precision(rest, 8, 7)
    return [high, mid, lax.reduce_precision(rest - mid, 8, 7)]


def near(halo, tfeat, index, shift, count, live, leaf_dev, rhs, slots):
    panels = halo.shape[2]
    whole = lambda *shape: pl.BlockSpec(shape, lambda l, *_: (0,) * len(shape))
    return pl.pallas_call(
        functools.partial(near_kernel, slots, leaf_dev),
        out_shape=jax.ShapeDtypeStruct((leaf_dev, rhs, panels), jnp.float32),
        grid_spec=pltpu.PrefetchScalarGridSpec(
            num_scalar_prefetch=4,
            grid=(leaf_dev,),
            in_specs=[
                whole(*halo.shape),
                pl.BlockSpec((1, 3, 16, panels), lambda l, *_: (l, 0, 0, 0)),
            ],
            out_specs=pl.BlockSpec((1, rhs, panels), lambda l, *_: (l, 0, 0)),
            scratch_shapes=[
                pltpu.VMEM((9 * leaf_dev, 16, panels), jnp.float32),
                pltpu.VMEM((9 * leaf_dev, panels), jnp.float32),
            ],
        ),
        compiler_params=pltpu.CompilerParams(vmem_limit_bytes=32 * 1024 * 1024),
    )(index, shift, count, live, halo, tfeat)


def body(sources, geometry, near_lists, far_lists, bases_in, bases_out, couplings):
    leaf_dev, rhs, panels = sources.shape[2:]
    slots = near_lists.shape[3]
    n_gx, n_gy = lax.axis_size("gx"), lax.axis_size("gy")
    row_pos, col_pos = lax.axis_index("gx"), lax.axis_index("gy")
    geo = geometry[0, 0]
    by_row = jnp.transpose(geo, (1, 0, 2)).reshape(4 * leaf_dev, panels)
    packed = jnp.concatenate([sources.reshape(leaf_dev * rhs, panels), by_row], axis=0)
    projection = jnp.einsum(
        "aqlp,lrp->aqr", bases_in[0, 0], sources[0, 0], preferred_element_type=jnp.float32
    )
    halo, target = exchange(
        packed, projection.reshape(128, rhs), couplings[0, 0], far_lists[0, 0], n_gx, n_gy
    )

    lists = near_lists[0, 0]
    live = lists >= 0
    own_leaf = jnp.arange(leaf_dev, dtype=jnp.int32)
    device = lists // leaf_dev
    src_leaf = lists % leaf_dev
    local = ((device // n_gy - row_pos + 1) * 3 + device % n_gy - col_pos + 1) * leaf_dev + src_leaf
    index = jnp.where(live, local, 4 * leaf_dev + own_leaf[:, None])
    shift = jnp.where(live, src_leaf - own_leaf[:, None] + 1, 1)
    count = jnp.sum(live.astype(jnp.int32), axis=1)

    t = geo.astype(jnp.float32)[:, None]
    tx, ty, tz = t[:, :, 0], t[:, :, 1], t[:, :, 2]
    dz = jnp.arange(-1, 2, dtype=jnp.float32)[None, :, None]
    shape = (leaf_dev, 3, panels)
    full = lambda v: jnp.broadcast_to(v, shape)
    one, zero = jnp.ones(shape, jnp.float32), jnp.zeros(shape, jnp.float32)
    p = tx * tx + ty * ty + (tz - dz) * (tz - dz)
    tfeat = jnp.stack(
        [full(v) for v in (-2 * tx, -2 * ty, -2 * tz, -2 * tx, -2 * ty, 2 * dz)]
        + pieces(p) + [one] * 3 + [zero] * 4,
        axis=2,
    ).astype(jnp.bfloat16)

    near_field = near(
        halo, tfeat,
        index.reshape(-1), shift.reshape(-1), count, live.astype(jnp.int32).reshape(-1),
        leaf_dev, rhs, slots,
    )
    far_field = jnp.einsum(
        "aqr,aqlp->lrp", target.reshape(4, 32, rhs), bases_out[0, 0],
        preferred_element_type=jnp.float32,
    )
    return (near_field + far_field).reshape(sources.shape)


def solution(mesh):
    in_specs = (
        P("gx", "gy", None, None, None),
        P("gx", "gy", None, None, None),
        P("gx", "gy", None, None),
        P("gx", "gy", None, None),
        P("gx", "gy", None, None, None, None),
        P("gx", "gy", None, None, None, None),
        P("gx", "gy", None, None, None),
    )
    out_specs = P("gx", "gy", None, None, None)
    return jax.shard_map(body, mesh=mesh, in_specs=in_specs, out_specs=out_specs, check_vma=False)
```

```python
import functools
import math

import jax
import jax.numpy as jnp
from jax import lax
from jax.experimental import pallas as pl
from jax.experimental.pallas import tpu as pltpu
from jax.sharding import PartitionSpec as P

FOUR_PI = 4.0 * math.pi
MESH = pl.DeviceIdType.MESH
UNROLL = 2


def exchange_kernel(
    n_gx, n_gy, packed, proj, coup, far, halo, target,
    col_buf, row_src, row_buf, tab3, gath, int_src, int_buf, c3_src, c3_buf,
    halo_s, halo_r, p1_s, p1_r, p2_s, p2_r, p3_s, p3_r, p4_s, p4_r,
):
    x = lax.axis_index("gx")
    y = lax.axis_index("gy")
    barrier = pltpu.get_barrier_semaphore()

    def inside(dx, dy):
        tests = []
        if dx == -1:
            tests.append(x > 0)
        if dx == 1:
            tests.append(x < n_gx - 1)
        if dy == -1:
            tests.append(y > 0)
        if dy == 1:
            tests.append(y < n_gy - 1)
        return functools.reduce(jnp.logical_and, tests)

    offsets = [(dx, dy) for dx in (-1, 0, 1) for dy in (-1, 0, 1) if (dx, dy) != (0, 0)]
    direct = [o for o in offsets if o[0] * o[1] == 0]
    diagonal = [o for o in offsets if o[0] * o[1] != 0]
    for k in range(1, n_gx):
        pl.semaphore_signal(
            barrier, inc=1, device_id=(lax.rem(x + k, n_gx), y), device_id_type=MESH
        )
    for k in range(1, n_gy):
        pl.semaphore_signal(
            barrier, inc=1, device_id=(x, lax.rem(y + k, n_gy)), device_id_type=MESH
        )
    pl.semaphore_wait(barrier, n_gx - 1 + n_gy - 1)

    def remote(src, dst, send, recv, where):
        return pltpu.make_async_remote_copy(
            src_ref=src, dst_ref=dst, send_sem=send, recv_sem=recv,
            device_id=where, device_id_type=MESH,
        )

    def column(src, buf, send, recv):
        for k in range(1, n_gy):
            to = lax.rem(y + k, n_gy)
            remote(src, buf.at[y], send.at[k], recv.at[y], (x, to)).start()
        buf[y] = src[...]

    def column_wait(src, buf, send, recv):
        for k in range(1, n_gy):
            peer = lax.rem(y + k, n_gy)
            remote(src, buf.at[peer], send.at[k], recv.at[peer], (x, peer)).wait_recv()

    def slot(dx, dy):
        return (dx + 1) * 3 + dy + 1

    def halo_copy(dx, dy):
        block = halo.at[slot(0, dy)] if dx != 0 and dy != 0 else packed
        there = slot(-dx, dy) if dx != 0 else slot(0, -dy)
        return remote(
            block, halo.at[there], halo_s.at[slot(dx, dy)], halo_r.at[there],
            (x + dx, y + dy if dx == 0 else y),
        )

    def halo_start(dx, dy):
        @pl.when(inside(dx, dy))
        def _():
            halo_copy(dx, dy).start()

    def halo_arrived(dx, dy):
        @pl.when(inside(dx, dy))
        def _():
            at = slot(dx, dy)
            origin = (x + dx, y) if dx != 0 else (x, y + dy)
            remote(packed, halo.at[at], halo_s.at[at], halo_r.at[at], origin).wait_recv()

    column(proj, col_buf, p1_s, p1_r)
    for dx, dy in direct:
        halo_start(dx, dy)
    halo[4] = packed[...]

    column_wait(proj, col_buf, p1_s, p1_r)
    quarter = 4 * (y // 4)
    half = target.shape[1]
    row_src[0:32, 0:half] = sum(col_buf[quarter + g, 32:64, 0:half] for g in range(4))
    coarse = sum(col_buf[g, :, half:] for g in range(n_gy))
    row_src[0:32, half:] = coarse[0:32]
    row_src[32:48, 0:half] = coarse[32:48]
    row_src[32:48, half:] = coarse[48:64]
    for k in range(1, n_gx):
        to = lax.rem(x + k, n_gx)
        remote(row_src, row_buf.at[x], p2_s.at[k], p2_r.at[x], (to, y)).start()
    row_buf[x] = row_src[...]
    for m in range(16):
        gath[pl.ds(m * 32, 32), :] = col_buf[far[0, m], 0:32, 0:half]
    first = jnp.dot(
        coup[0], gath[...], preferred_element_type=jnp.float32, precision=lax.Precision.HIGHEST
    )
    target[0:32, :] = first.astype(jnp.bfloat16)
    for k in range(1, n_gx):
        peer = lax.rem(x + k, n_gx)
        remote(row_src, row_buf.at[peer], p2_s.at[k], p2_r.at[peer], (peer, y)).wait_recv()
    for dy in (-1, 1):
        halo_arrived(0, dy)
    for dx, dy in diagonal:
        halo_start(dx, dy)
    for c in range(n_gx // 4):
        coarse = sum(row_buf[4 * c + g, 32:48, :] for g in range(4))
        tab3[c, 0:16, :] = coarse[:, 0:half]
        tab3[c, 16:32, :] = coarse[:, half:]
    for level in (1, 2, 3):
        for m in range(16):
            s = far[level, m]
            if level == 3:
                gath[pl.ds(m * 32, 32), :] = tab3[s]
            elif level == 1:
                gath[pl.ds(m * 32, 32), :] = row_buf[s, 0:32, 0:half]
            else:
                gath[pl.ds(m * 32, 32), :] = row_buf[s, 0:32, half:]
        term = jnp.dot(
            coup[level], gath[...], preferred_element_type=jnp.float32,
            precision=lax.Precision.HIGHEST,
        )
        if level == 1:
            int_src[0:32, 0:half] = term
        elif level == 2:
            int_src[0:32, half:] = term
        else:
            int_src[32:48, 0:half] = term[0:16]
            int_src[32:48, half:] = term[16:32]
    column(int_src, int_buf, p3_s, p3_r)
    column_wait(int_src, int_buf, p3_s, p3_r)
    c3_src[...] = sum(int_buf[g, 32:48, :] for g in range(n_gy))
    base = 4 * (x // 4)
    spot = lax.rem(x, 4)
    for k in range(1, 4):
        to = base + lax.rem(spot + k, 4)
        remote(c3_src, c3_buf.at[spot], p4_s.at[k], p4_r.at[spot], (to, y)).start()
    c3_buf[spot] = c3_src[...]
    target[32:64, :] = sum(int_buf[quarter + g, 0:32, 0:half] for g in range(4)).astype(jnp.bfloat16)
    target[64:96, :] = sum(int_buf[g, 0:32, half:] for g in range(n_gy)).astype(jnp.bfloat16)
    for k in range(1, 4):
        peer = lax.rem(spot + k, 4)
        remote(c3_src, c3_buf.at[peer], p4_s.at[k], p4_r.at[peer], (base + peer, y)).wait_recv()
    coarse = sum(c3_buf[g] for g in range(4)).astype(jnp.bfloat16)
    target[96:112, :] = coarse[:, 0:half]
    target[112:128, :] = coarse[:, half:]

    for dx, dy in offsets:
        if dx != 0:
            halo_arrived(dx, dy)

        @pl.when(inside(dx, dy))
        def _():
            halo_copy(dx, dy).wait_send()

    for k in range(1, n_gy):
        to = lax.rem(y + k, n_gy)
        remote(proj, col_buf.at[y], p1_s.at[k], p1_r.at[y], (x, to)).wait_send()
        remote(int_src, int_buf.at[y], p3_s.at[k], p3_r.at[y], (x, to)).wait_send()
    for k in range(1, n_gx):
        to = lax.rem(x + k, n_gx)
        remote(row_src, row_buf.at[x], p2_s.at[k], p2_r.at[x], (to, y)).wait_send()
    for k in range(1, 4):
        to = base + lax.rem(spot + k, 4)
        remote(c3_src, c3_buf.at[spot], p4_s.at[k], p4_r.at[spot], (to, y)).wait_send()


def exchange(packed, proj, coup, far, n_gx, n_gy):
    rows, panels = packed.shape
    rhs = proj.shape[1] // 2
    vmem = pl.BlockSpec(memory_space=pltpu.VMEM)
    f32 = jnp.float32
    sems = pltpu.SemaphoreType.DMA
    return pl.pallas_call(
        functools.partial(exchange_kernel, n_gx, n_gy),
        out_shape=(
            jax.ShapeDtypeStruct((9, rows, panels), jnp.bfloat16),
            jax.ShapeDtypeStruct((128, rhs), jnp.bfloat16),
        ),
        in_specs=[vmem, vmem, vmem, pl.BlockSpec(memory_space=pltpu.SMEM)],
        out_specs=(vmem, vmem),
        scratch_shapes=[
            pltpu.VMEM((n_gy, 64, 2 * rhs), f32),
            pltpu.VMEM((48, 2 * rhs), f32),
            pltpu.VMEM((n_gx, 48, 2 * rhs), f32),
            pltpu.VMEM((n_gx // 4, 32, rhs), f32),
            pltpu.VMEM((512, rhs), f32),
            pltpu.VMEM((48, 2 * rhs), f32),
            pltpu.VMEM((n_gy, 48, 2 * rhs), f32),
            pltpu.VMEM((16, 2 * rhs), f32),
            pltpu.VMEM((4, 16, 2 * rhs), f32),
            sems((9,)), sems((9,)),
            sems((n_gy,)), sems((n_gy,)),
            sems((n_gx,)), sems((n_gx,)),
            sems((n_gy,)), sems((n_gy,)),
            sems((4,)), sems((4,)),
        ],
        compiler_params=pltpu.CompilerParams(
            collective_id=0, has_side_effects=True, vmem_limit_bytes=32 * 1024 * 1024
        ),
    )(packed, proj, coup, far)


def near_kernel(slots, leaf_dev, index, shift, count, live, halo, tfeat, out, sfeat, scale):
    leaf = pl.program_id(0)
    rhs = out.shape[1]

    @pl.when(leaf == 0)
    def _():
        def source_features(place, carry):
            def row(c):
                wide = halo[place, pl.ds(leaf_dev * rhs, 4 * leaf_dev), :].astype(jnp.float32)
                return wide[c * leaf_dev : (c + 1) * leaf_dev]

            sx, sy, sz, area = row(0), row(1), row(2), row(3)
            dx = (place // 3 - 1).astype(jnp.float32)
            dy = (lax.rem(place, 3) - 1).astype(jnp.float32)
            q = (sx + dx) * (sx + dx) + (sy + dy) * (sy + dy) + sz * sz + area
            high = q.astype(jnp.bfloat16).astype(jnp.float32)
            mid = (q - high).astype(jnp.bfloat16).astype(jnp.float32)
            one, zero = jnp.ones_like(q), jnp.zeros_like(q)
            rows = [sx, sy, sz, dx + zero, dy + zero, sz, one, one, one]
            rows += [high, mid, q - high - mid] + [zero] * 4
            own = pl.ds(pl.multiple_of(place * leaf_dev, leaf_dev), leaf_dev)
            for k, value in enumerate(rows):
                sfeat[own, k, :] = value
            scale[own, :] = area * (1.0 / FOUR_PI)
            return carry

        lax.fori_loop(0, 9, source_features, 0)

    out[0] = jnp.zeros(out.shape[1:], jnp.float32)

    def step(pair, carry):
        total = None
        for u in range(UNROLL):
            at = leaf * slots + pair * UNROLL + u
            n = index[at]
            squared = lax.dot_general(
                tfeat[0, shift[at]], sfeat[n].astype(jnp.bfloat16), (((0,), (0,)), ((), ())),
                preferred_element_type=jnp.float32,
            )
            weight = scale[pl.ds(n, 1), :] * live[at].astype(jnp.float32)
            kernel = (lax.rsqrt(squared) * weight).astype(jnp.bfloat16)
            src = halo[n // 8, pl.ds(pl.multiple_of(lax.rem(n, 8) * rhs, rhs), rhs), :]
            term = lax.dot_general(
                src, kernel, (((1,), (1,)), ((), ())), preferred_element_type=jnp.float32
            )
            total = term if total is None else total + term
        out[0] += total
        return carry

    lax.fori_loop(0, (count[leaf] + UNROLL - 1) // UNROLL, step, 0)


def pieces(v):
    high = lax.reduce_precision(v, 8, 7)
    rest = v - high
    mid = lax.reduce_precision(rest, 8, 7)
    return [high, mid, lax.reduce_precision(rest - mid, 8, 7)]


def near(halo, tfeat, index, shift, count, live, leaf_dev, rhs, slots):
    panels = halo.shape[2]
    whole = lambda *shape: pl.BlockSpec(shape, lambda l, *_: (0,) * len(shape))
    return pl.pallas_call(
        functools.partial(near_kernel, slots, leaf_dev),
        out_shape=jax.ShapeDtypeStruct((leaf_dev, rhs, panels), jnp.float32),
        grid_spec=pltpu.PrefetchScalarGridSpec(
            num_scalar_prefetch=4,
            grid=(leaf_dev,),
            in_specs=[
                whole(*halo.shape),
                pl.BlockSpec((1, 3, 16, panels), lambda l, *_: (l, 0, 0, 0)),
            ],
            out_specs=pl.BlockSpec((1, rhs, panels), lambda l, *_: (l, 0, 0)),
            scratch_shapes=[
                pltpu.VMEM((9 * leaf_dev, 16, panels), jnp.float32),
                pltpu.VMEM((9 * leaf_dev, panels), jnp.float32),
            ],
        ),
        compiler_params=pltpu.CompilerParams(vmem_limit_bytes=32 * 1024 * 1024),
    )(index, shift, count, live, halo, tfeat)


def body(sources, geometry, near_lists, far_lists, bases_in, bases_out, couplings):
    leaf_dev, rhs, panels = sources.shape[2:]
    slots = near_lists.shape[3]
    n_gx, n_gy = lax.axis_size("gx"), lax.axis_size("gy")
    row_pos, col_pos = lax.axis_index("gx"), lax.axis_index("gy")
    geo = geometry[0, 0]
    by_row = jnp.transpose(geo, (1, 0, 2)).reshape(4 * leaf_dev, panels)
    packed = jnp.concatenate([sources.reshape(leaf_dev * rhs, panels), by_row], axis=0)
    projection = jnp.einsum(
        "aqlp,lrp->aqr", bases_in[0, 0], sources[0, 0], preferred_element_type=jnp.float32
    )
    level_pairs = projection.reshape(2, 64, rhs)
    halo, target = exchange(
        packed, jnp.concatenate([level_pairs[0], level_pairs[1]], axis=1), couplings[0, 0], far_lists[0, 0], n_gx, n_gy
    )

    lists = near_lists[0, 0]
    live = lists >= 0
    own_leaf = jnp.arange(leaf_dev, dtype=jnp.int32)
    device = lists // leaf_dev
    src_leaf = lists % leaf_dev
    local = ((device // n_gy - row_pos + 1) * 3 + device % n_gy - col_pos + 1) * leaf_dev + src_leaf
    index = jnp.where(live, local, 4 * leaf_dev + own_leaf[:, None])
    shift = jnp.where(live, src_leaf - own_leaf[:, None] + 1, 1)
    count = jnp.sum(live.astype(jnp.int32), axis=1)

    t = geo.astype(jnp.float32)[:, None]
    tx, ty, tz = t[:, :, 0], t[:, :, 1], t[:, :, 2]
    dz = jnp.arange(-1, 2, dtype=jnp.float32)[None, :, None]
    shape = (leaf_dev, 3, panels)
    full = lambda v: jnp.broadcast_to(v, shape)
    one, zero = jnp.ones(shape, jnp.float32), jnp.zeros(shape, jnp.float32)
    p = tx * tx + ty * ty + (tz - dz) * (tz - dz)
    tfeat = jnp.stack(
        [full(v) for v in (-2 * tx, -2 * ty, -2 * tz, -2 * tx, -2 * ty, 2 * dz)]
        + pieces(p) + [one] * 3 + [zero] * 4,
        axis=2,
    ).astype(jnp.bfloat16)

    near_field = near(
        halo, tfeat,
        index.reshape(-1), shift.reshape(-1), count, live.astype(jnp.int32).reshape(-1),
        leaf_dev, rhs, slots,
    )
    far_field = jnp.einsum(
        "aqr,aqlp->lrp", target.reshape(4, 32, rhs), bases_out[0, 0],
        preferred_element_type=jnp.float32,
    )
    return (near_field + far_field).reshape(sources.shape)


def solution(mesh):
    in_specs = (
        P("gx", "gy", None, None, None),
        P("gx", "gy", None, None, None),
        P("gx", "gy", None, None),
        P("gx", "gy", None, None),
        P("gx", "gy", None, None, None, None),
        P("gx", "gy", None, None, None, None),
        P("gx", "gy", None, None, None),
    )
    out_specs = P("gx", "gy", None, None, None)
    return jax.shard_map(body, mesh=mesh, in_specs=in_specs, out_specs=out_specs, check_vma=False)
```

```python
import functools
import math

import jax
import jax.numpy as jnp
from jax import lax
from jax.experimental import pallas as pl
from jax.experimental.pallas import tpu as pltpu
from jax.sharding import PartitionSpec as P

FOUR_PI = 4.0 * math.pi
MESH = pl.DeviceIdType.MESH
UNROLL = 4
FEATURES = 32


def exchange_kernel(
    n_gx, n_gy, packed, proj, coup, far, halo, target,
    col_buf, row_src, row_buf, tab3, gath, int_src, int_buf, c3_src, c3_buf,
    halo_s, halo_r, p1_s, p1_r, p2_s, p2_r, p3_s, p3_r, p4_s, p4_r,
):
    x = lax.axis_index("gx")
    y = lax.axis_index("gy")
    barrier = pltpu.get_barrier_semaphore()

    def inside(dx, dy):
        tests = []
        if dx == -1:
            tests.append(x > 0)
        if dx == 1:
            tests.append(x < n_gx - 1)
        if dy == -1:
            tests.append(y > 0)
        if dy == 1:
            tests.append(y < n_gy - 1)
        return functools.reduce(jnp.logical_and, tests)

    offsets = [(dx, dy) for dx in (-1, 0, 1) for dy in (-1, 0, 1) if (dx, dy) != (0, 0)]
    direct = [o for o in offsets if o[0] * o[1] == 0]
    diagonal = [o for o in offsets if o[0] * o[1] != 0]
    for k in range(1, n_gx):
        pl.semaphore_signal(
            barrier, inc=1, device_id=(lax.rem(x + k, n_gx), y), device_id_type=MESH
        )
    for k in range(1, n_gy):
        pl.semaphore_signal(
            barrier, inc=1, device_id=(x, lax.rem(y + k, n_gy)), device_id_type=MESH
        )
    pl.semaphore_wait(barrier, n_gx - 1 + n_gy - 1)

    def remote(src, dst, send, recv, where):
        return pltpu.make_async_remote_copy(
            src_ref=src, dst_ref=dst, send_sem=send, recv_sem=recv,
            device_id=where, device_id_type=MESH,
        )

    def column(src, buf, send, recv):
        for k in range(1, n_gy):
            to = lax.rem(y + k, n_gy)
            remote(src, buf.at[y], send.at[k], recv.at[y], (x, to)).start()
        buf[y] = src[...]

    def column_wait(src, buf, send, recv):
        for k in range(1, n_gy):
            peer = lax.rem(y + k, n_gy)
            remote(src, buf.at[peer], send.at[k], recv.at[peer], (x, peer)).wait_recv()

    def slot(dx, dy):
        return (dx + 1) * 3 + dy + 1

    def halo_copy(dx, dy):
        block = halo.at[slot(0, dy)] if dx != 0 and dy != 0 else packed
        there = slot(-dx, dy) if dx != 0 else slot(0, -dy)
        return remote(
            block, halo.at[there], halo_s.at[slot(dx, dy)], halo_r.at[there],
            (x + dx, y + dy if dx == 0 else y),
        )

    def halo_start(dx, dy):
        @pl.when(inside(dx, dy))
        def _():
            halo_copy(dx, dy).start()

    def halo_arrived(dx, dy):
        @pl.when(inside(dx, dy))
        def _():
            at = slot(dx, dy)
            origin = (x + dx, y) if dx != 0 else (x, y + dy)
            remote(packed, halo.at[at], halo_s.at[at], halo_r.at[at], origin).wait_recv()

    column(proj, col_buf, p1_s, p1_r)
    for dx, dy in direct:
        halo_start(dx, dy)
    halo[4] = packed[...]

    column_wait(proj, col_buf, p1_s, p1_r)
    quarter = 4 * (y // 4)
    half = target.shape[1]
    row_src[0:32, 0:half] = sum(col_buf[quarter + g, 32:64, 0:half] for g in range(4))
    coarse = sum(col_buf[g, :, half:] for g in range(n_gy))
    row_src[0:32, half:] = coarse[0:32]
    row_src[32:48, 0:half] = coarse[32:48]
    row_src[32:48, half:] = coarse[48:64]
    for k in range(1, n_gx):
        to = lax.rem(x + k, n_gx)
        remote(row_src, row_buf.at[x], p2_s.at[k], p2_r.at[x], (to, y)).start()
    row_buf[x] = row_src[...]
    for m in range(16):
        gath[pl.ds(m * 32, 32), :] = col_buf[far[0, m], 0:32, 0:half]
    first = jnp.dot(
        coup[0], gath[...], preferred_element_type=jnp.float32, precision=lax.Precision.HIGHEST
    )
    target[0:32, :] = first.astype(jnp.bfloat16)
    for k in range(1, n_gx):
        peer = lax.rem(x + k, n_gx)
        remote(row_src, row_buf.at[peer], p2_s.at[k], p2_r.at[peer], (peer, y)).wait_recv()
    for dy in (-1, 1):
        halo_arrived(0, dy)
    for dx, dy in diagonal:
        halo_start(dx, dy)
    for c in range(n_gx // 4):
        coarse = sum(row_buf[4 * c + g, 32:48, :] for g in range(4))
        tab3[c, 0:16, :] = coarse[:, 0:half]
        tab3[c, 16:32, :] = coarse[:, half:]
    for level in (1, 2, 3):
        for m in range(16):
            s = far[level, m]
            if level == 3:
                gath[pl.ds(m * 32, 32), :] = tab3[s]
            elif level == 1:
                gath[pl.ds(m * 32, 32), :] = row_buf[s, 0:32, 0:half]
            else:
                gath[pl.ds(m * 32, 32), :] = row_buf[s, 0:32, half:]
        term = jnp.dot(
            coup[level], gath[...], preferred_element_type=jnp.float32,
            precision=lax.Precision.HIGHEST,
        )
        if level == 1:
            int_src[0:32, 0:half] = term
        elif level == 2:
            int_src[0:32, half:] = term
        else:
            int_src[32:48, 0:half] = term[0:16]
            int_src[32:48, half:] = term[16:32]
    column(int_src, int_buf, p3_s, p3_r)
    column_wait(int_src, int_buf, p3_s, p3_r)
    c3_src[...] = sum(int_buf[g, 32:48, :] for g in range(n_gy))
    base = 4 * (x // 4)
    spot = lax.rem(x, 4)
    for k in range(1, 4):
        to = base + lax.rem(spot + k, 4)
        remote(c3_src, c3_buf.at[spot], p4_s.at[k], p4_r.at[spot], (to, y)).start()
    c3_buf[spot] = c3_src[...]
    target[32:64, :] = sum(int_buf[quarter + g, 0:32, 0:half] for g in range(4)).astype(jnp.bfloat16)
    target[64:96, :] = sum(int_buf[g, 0:32, half:] for g in range(n_gy)).astype(jnp.bfloat16)
    for k in range(1, 4):
        peer = lax.rem(spot + k, 4)
        remote(c3_src, c3_buf.at[peer], p4_s.at[k], p4_r.at[peer], (base + peer, y)).wait_recv()
    coarse = sum(c3_buf[g] for g in range(4)).astype(jnp.bfloat16)
    target[96:112, :] = coarse[:, 0:half]
    target[112:128, :] = coarse[:, half:]

    for dx, dy in offsets:
        if dx != 0:
            halo_arrived(dx, dy)

        @pl.when(inside(dx, dy))
        def _():
            halo_copy(dx, dy).wait_send()

    for k in range(1, n_gy):
        to = lax.rem(y + k, n_gy)
        remote(proj, col_buf.at[y], p1_s.at[k], p1_r.at[y], (x, to)).wait_send()
        remote(int_src, int_buf.at[y], p3_s.at[k], p3_r.at[y], (x, to)).wait_send()
    for k in range(1, n_gx):
        to = lax.rem(x + k, n_gx)
        remote(row_src, row_buf.at[x], p2_s.at[k], p2_r.at[x], (to, y)).wait_send()
    for k in range(1, 4):
        to = base + lax.rem(spot + k, 4)
        remote(c3_src, c3_buf.at[spot], p4_s.at[k], p4_r.at[spot], (to, y)).wait_send()


def exchange(packed, proj, coup, far, n_gx, n_gy):
    rows, panels = packed.shape
    rhs = proj.shape[1] // 2
    vmem = pl.BlockSpec(memory_space=pltpu.VMEM)
    f32 = jnp.float32
    sems = pltpu.SemaphoreType.DMA
    return pl.pallas_call(
        functools.partial(exchange_kernel, n_gx, n_gy),
        out_shape=(
            jax.ShapeDtypeStruct((9, rows, panels), jnp.bfloat16),
            jax.ShapeDtypeStruct((128, rhs), jnp.bfloat16),
        ),
        in_specs=[vmem, vmem, vmem, pl.BlockSpec(memory_space=pltpu.SMEM)],
        out_specs=(vmem, vmem),
        scratch_shapes=[
            pltpu.VMEM((n_gy, 64, 2 * rhs), f32),
            pltpu.VMEM((48, 2 * rhs), f32),
            pltpu.VMEM((n_gx, 48, 2 * rhs), f32),
            pltpu.VMEM((n_gx // 4, 32, rhs), f32),
            pltpu.VMEM((512, rhs), f32),
            pltpu.VMEM((48, 2 * rhs), f32),
            pltpu.VMEM((n_gy, 48, 2 * rhs), f32),
            pltpu.VMEM((16, 2 * rhs), f32),
            pltpu.VMEM((4, 16, 2 * rhs), f32),
            sems((9,)), sems((9,)),
            sems((n_gy,)), sems((n_gy,)),
            sems((n_gx,)), sems((n_gx,)),
            sems((n_gy,)), sems((n_gy,)),
            sems((4,)), sems((4,)),
        ],
        compiler_params=pltpu.CompilerParams(
            collective_id=0, has_side_effects=True, vmem_limit_bytes=32 * 1024 * 1024
        ),
    )(packed, proj, coup, far)


def near_kernel(slots, leaf_dev, index, shift, count, live, halo, tfeat, out, sfeat):
    leaf = pl.program_id(0)
    rhs = out.shape[1]

    @pl.when(leaf == 0)
    def _():
        def source_features(place, carry):
            def row(c):
                wide = halo[place, pl.ds(leaf_dev * rhs, 4 * leaf_dev), :].astype(jnp.float32)
                return wide[c * leaf_dev : (c + 1) * leaf_dev]

            sx, sy, sz, area = row(0), row(1), row(2), row(3)
            dx = (place // 3 - 1).astype(jnp.float32)
            dy = (lax.rem(place, 3) - 1).astype(jnp.float32)
            sx, sy = sx + dx, sy + dy
            factor = FOUR_PI / area
            factor = factor * factor

            def split(v):
                high = v.astype(jnp.bfloat16).astype(jnp.float32)
                mid = (v - high).astype(jnp.bfloat16).astype(jnp.float32)
                return [high, mid, v - high - mid]

            high, mid, low = split(factor)
            along_z = split(factor * sz)
            rows = split(factor * sx) + split(factor * sy) + along_z + along_z
            rows += [high, high, high, mid, mid, low]
            rows += split(factor * (sx * sx + sy * sy + sz * sz + area))
            rows += [jnp.zeros_like(factor)] * (FEATURES - len(rows))
            own = pl.ds(pl.multiple_of(place * leaf_dev, leaf_dev), leaf_dev)
            for k, value in enumerate(rows):
                sfeat[own, k, :] = value
            return carry

        lax.fori_loop(0, 9, source_features, 0)

    out[0] = jnp.zeros(out.shape[1:], jnp.float32)

    def step(pair, carry):
        total = None
        for u in range(UNROLL):
            at = leaf * slots + pair * UNROLL + u
            n = index[at]
            squared = lax.dot_general(
                sfeat[n].astype(jnp.bfloat16), tfeat[0, shift[at]], (((0,), (0,)), ((), ())),
                preferred_element_type=jnp.float32,
            )
            kernel = lax.rsqrt(squared).astype(jnp.bfloat16)
            src = halo[n // 8, pl.ds(pl.multiple_of(lax.rem(n, 8) * rhs, rhs), rhs), :]
            term = lax.dot_general(
                src * live[at].astype(jnp.bfloat16), kernel, (((1,), (0,)), ((), ())),
                preferred_element_type=jnp.float32,
            )
            total = term if total is None else total + term
        out[0] += total
        return carry

    lax.fori_loop(0, (count[leaf] + UNROLL - 1) // UNROLL, step, 0)


def pieces(v):
    high = lax.reduce_precision(v, 8, 7)
    rest = v - high
    mid = lax.reduce_precision(rest, 8, 7)
    return [high, mid, lax.reduce_precision(rest - mid, 8, 7)]


def near(halo, tfeat, index, shift, count, live, leaf_dev, rhs, slots):
    panels = halo.shape[2]
    whole = lambda *shape: pl.BlockSpec(shape, lambda l, *_: (0,) * len(shape))
    return pl.pallas_call(
        functools.partial(near_kernel, slots, leaf_dev),
        out_shape=jax.ShapeDtypeStruct((leaf_dev, rhs, panels), jnp.float32),
        grid_spec=pltpu.PrefetchScalarGridSpec(
            num_scalar_prefetch=4,
            grid=(leaf_dev,),
            in_specs=[
                whole(*halo.shape),
                pl.BlockSpec((1, 3, FEATURES, panels), lambda l, *_: (l, 0, 0, 0)),
            ],
            out_specs=pl.BlockSpec((1, rhs, panels), lambda l, *_: (l, 0, 0)),
            scratch_shapes=[
                pltpu.VMEM((9 * leaf_dev, FEATURES, panels), jnp.float32),
            ],
        ),
        compiler_params=pltpu.CompilerParams(vmem_limit_bytes=32 * 1024 * 1024),
    )(index, shift, count, live, halo, tfeat)


def body(sources, geometry, near_lists, far_lists, bases_in, bases_out, couplings):
    leaf_dev, rhs, panels = sources.shape[2:]
    slots = near_lists.shape[3]
    n_gx, n_gy = lax.axis_size("gx"), lax.axis_size("gy")
    row_pos, col_pos = lax.axis_index("gx"), lax.axis_index("gy")
    geo = geometry[0, 0]
    by_row = jnp.transpose(geo, (1, 0, 2)).reshape(4 * leaf_dev, panels)
    packed = jnp.concatenate([sources.reshape(leaf_dev * rhs, panels), by_row], axis=0)
    projection = jnp.einsum(
        "aqlp,lrp->aqr", bases_in[0, 0], sources[0, 0], preferred_element_type=jnp.float32
    )
    level_pairs = projection.reshape(2, 64, rhs)
    halo, target = exchange(
        packed, jnp.concatenate([level_pairs[0], level_pairs[1]], axis=1), couplings[0, 0], far_lists[0, 0], n_gx, n_gy
    )

    lists = near_lists[0, 0]
    live = lists >= 0
    own_leaf = jnp.arange(leaf_dev, dtype=jnp.int32)
    device = lists // leaf_dev
    src_leaf = lists % leaf_dev
    local = ((device // n_gy - row_pos + 1) * 3 + device % n_gy - col_pos + 1) * leaf_dev + src_leaf
    index = jnp.where(live, local, 4 * leaf_dev + own_leaf[:, None])
    shift = jnp.where(live, src_leaf - own_leaf[:, None] + 1, 1)
    count = jnp.sum(live.astype(jnp.int32), axis=1)

    t = geo.astype(jnp.float32)[:, None]
    tx, ty, tz = t[:, :, 0], t[:, :, 1], t[:, :, 2]
    dz = jnp.arange(-1, 2, dtype=jnp.float32)[None, :, None]
    shape = (leaf_dev, 3, panels)
    full = lambda v: jnp.broadcast_to(v, shape)
    one, zero = jnp.ones(shape, jnp.float32), jnp.zeros(shape, jnp.float32)
    p = tx * tx + ty * ty + (tz - dz) * (tz - dz)
    high, mid, low = pieces(p)
    rows = [full(-2 * tx)] * 3 + [full(-2 * ty)] * 3 + [full(-2 * tz)] * 3 + [full(2 * dz)] * 3
    rows += [high, mid, low, high, mid, high] + [one] * 3
    rows += [zero] * (FEATURES - len(rows))
    tfeat = jnp.stack(rows, axis=2).astype(jnp.bfloat16)

    near_field = near(
        halo, tfeat,
        index.reshape(-1), shift.reshape(-1), count, live.astype(jnp.int32).reshape(-1),
        leaf_dev, rhs, slots,
    )
    far_field = jnp.einsum(
        "aqr,aqlp->lrp", target.reshape(4, 32, rhs), bases_out[0, 0],
        preferred_element_type=jnp.float32,
    )
    return (near_field + far_field).reshape(sources.shape)


def solution(mesh):
    in_specs = (
        P("gx", "gy", None, None, None),
        P("gx", "gy", None, None, None),
        P("gx", "gy", None, None),
        P("gx", "gy", None, None),
        P("gx", "gy", None, None, None, None),
        P("gx", "gy", None, None, None, None),
        P("gx", "gy", None, None, None),
    )
    out_specs = P("gx", "gy", None, None, None)
    return jax.shard_map(body, mesh=mesh, in_specs=in_specs, out_specs=out_specs, check_vma=False)
```

```python
import functools
import math

import jax
import jax.numpy as jnp
from jax import lax
from jax.experimental import pallas as pl
from jax.experimental.pallas import tpu as pltpu
from jax.sharding import PartitionSpec as P

FOUR_PI = 4.0 * math.pi
MESH = pl.DeviceIdType.MESH
UNROLL = 4
FEATURES = 32


def exchange_kernel(
    n_gx, n_gy, packed, proj, coup, far, halo, target,
    col_buf, row_src, row_buf, tab3, gath, int_src, int_buf, c3_src, c3_buf,
    halo_s, halo_r, p1_s, p1_r, p2_s, p2_r, p3_s, p3_r, p4_s, p4_r,
):
    x = lax.axis_index("gx")
    y = lax.axis_index("gy")
    barrier = pltpu.get_barrier_semaphore()

    def inside(dx, dy):
        tests = []
        if dx == -1:
            tests.append(x > 0)
        if dx == 1:
            tests.append(x < n_gx - 1)
        if dy == -1:
            tests.append(y > 0)
        if dy == 1:
            tests.append(y < n_gy - 1)
        return functools.reduce(jnp.logical_and, tests)

    offsets = [(dx, dy) for dx in (-1, 0, 1) for dy in (-1, 0, 1) if (dx, dy) != (0, 0)]
    direct = [o for o in offsets if o[0] * o[1] == 0]
    diagonal = [o for o in offsets if o[0] * o[1] != 0]
    for k in range(1, n_gx):
        pl.semaphore_signal(
            barrier, inc=1, device_id=(lax.rem(x + k, n_gx), y), device_id_type=MESH
        )
    for k in range(1, n_gy):
        pl.semaphore_signal(
            barrier, inc=1, device_id=(x, lax.rem(y + k, n_gy)), device_id_type=MESH
        )
    pl.semaphore_wait(barrier, n_gx - 1 + n_gy - 1)

    def remote(src, dst, send, recv, where):
        return pltpu.make_async_remote_copy(
            src_ref=src, dst_ref=dst, send_sem=send, recv_sem=recv,
            device_id=where, device_id_type=MESH,
        )

    def column(src, buf, send, recv):
        for k in range(1, n_gy):
            to = lax.rem(y + k, n_gy)
            remote(src, buf.at[y], send.at[k], recv.at[y], (x, to)).start()
        buf[y] = src[...]

    def column_wait(src, buf, send, recv):
        for k in range(1, n_gy):
            peer = lax.rem(y + k, n_gy)
            remote(src, buf.at[peer], send.at[k], recv.at[peer], (x, peer)).wait_recv()

    def slot(dx, dy):
        return (dx + 1) * 3 + dy + 1

    def halo_copy(dx, dy):
        block = halo.at[slot(0, dy)] if dx != 0 and dy != 0 else packed
        there = slot(-dx, dy) if dx != 0 else slot(0, -dy)
        return remote(
            block, halo.at[there], halo_s.at[slot(dx, dy)], halo_r.at[there],
            (x + dx, y + dy if dx == 0 else y),
        )

    def halo_start(dx, dy):
        @pl.when(inside(dx, dy))
        def _():
            halo_copy(dx, dy).start()

    def halo_arrived(dx, dy):
        @pl.when(inside(dx, dy))
        def _():
            at = slot(dx, dy)
            origin = (x + dx, y) if dx != 0 else (x, y + dy)
            remote(packed, halo.at[at], halo_s.at[at], halo_r.at[at], origin).wait_recv()

    column(proj, col_buf, p1_s, p1_r)
    for dx, dy in direct:
        halo_start(dx, dy)
    halo[4] = packed[...]

    column_wait(proj, col_buf, p1_s, p1_r)
    quarter = 4 * (y // 4)
    half = target.shape[1]
    row_src[0:32, 0:half] = sum(col_buf[quarter + g, 32:64, 0:half] for g in range(4))
    coarse = sum(col_buf[g, :, half:] for g in range(n_gy))
    row_src[0:32, half:] = coarse[0:32]
    row_src[32:48, 0:half] = coarse[32:48]
    row_src[32:48, half:] = coarse[48:64]
    for k in range(1, n_gx):
        to = lax.rem(x + k, n_gx)
        remote(row_src, row_buf.at[x], p2_s.at[k], p2_r.at[x], (to, y)).start()
    row_buf[x] = row_src[...]
    for m in range(16):
        gath[pl.ds(m * 32, 32), :] = col_buf[far[0, m], 0:32, 0:half]
    first = jnp.dot(
        coup[0], gath[...], preferred_element_type=jnp.float32, precision=lax.Precision.HIGHEST
    )
    target[0:32, :] = first.astype(jnp.bfloat16)
    for dy in (-1, 1):
        halo_arrived(0, dy)
    for dx, dy in diagonal:
        halo_start(dx, dy)
    for k in range(1, n_gx):
        peer = lax.rem(x + k, n_gx)
        remote(row_src, row_buf.at[peer], p2_s.at[k], p2_r.at[peer], (peer, y)).wait_recv()
    for c in range(n_gx // 4):
        coarse = sum(row_buf[4 * c + g, 32:48, :] for g in range(4))
        tab3[c, 0:16, :] = coarse[:, 0:half]
        tab3[c, 16:32, :] = coarse[:, half:]
    for level in (1, 2, 3):
        for m in range(16):
            s = far[level, m]
            if level == 3:
                gath[pl.ds(m * 32, 32), :] = tab3[s]
            elif level == 1:
                gath[pl.ds(m * 32, 32), :] = row_buf[s, 0:32, 0:half]
            else:
                gath[pl.ds(m * 32, 32), :] = row_buf[s, 0:32, half:]
        term = jnp.dot(
            coup[level], gath[...], preferred_element_type=jnp.float32,
            precision=lax.Precision.HIGHEST,
        )
        if level == 1:
            int_src[0:32, 0:half] = term
        elif level == 2:
            int_src[0:32, half:] = term
        else:
            int_src[32:48, 0:half] = term[0:16]
            int_src[32:48, half:] = term[16:32]
    column(int_src, int_buf, p3_s, p3_r)
    column_wait(int_src, int_buf, p3_s, p3_r)
    c3_src[...] = sum(int_buf[g, 32:48, :] for g in range(n_gy))
    base = 4 * (x // 4)
    spot = lax.rem(x, 4)
    for k in range(1, 4):
        to = base + lax.rem(spot + k, 4)
        remote(c3_src, c3_buf.at[spot], p4_s.at[k], p4_r.at[spot], (to, y)).start()
    c3_buf[spot] = c3_src[...]
    target[32:64, :] = sum(int_buf[quarter + g, 0:32, 0:half] for g in range(4)).astype(jnp.bfloat16)
    target[64:96, :] = sum(int_buf[g, 0:32, half:] for g in range(n_gy)).astype(jnp.bfloat16)
    for k in range(1, 4):
        peer = lax.rem(spot + k, 4)
        remote(c3_src, c3_buf.at[peer], p4_s.at[k], p4_r.at[peer], (base + peer, y)).wait_recv()
    coarse = sum(c3_buf[g] for g in range(4)).astype(jnp.bfloat16)
    target[96:112, :] = coarse[:, 0:half]
    target[112:128, :] = coarse[:, half:]

    for dx, dy in offsets:
        if dx != 0:
            halo_arrived(dx, dy)

        @pl.when(inside(dx, dy))
        def _():
            halo_copy(dx, dy).wait_send()

    for k in range(1, n_gy):
        to = lax.rem(y + k, n_gy)
        remote(proj, col_buf.at[y], p1_s.at[k], p1_r.at[y], (x, to)).wait_send()
        remote(int_src, int_buf.at[y], p3_s.at[k], p3_r.at[y], (x, to)).wait_send()
    for k in range(1, n_gx):
        to = lax.rem(x + k, n_gx)
        remote(row_src, row_buf.at[x], p2_s.at[k], p2_r.at[x], (to, y)).wait_send()
    for k in range(1, 4):
        to = base + lax.rem(spot + k, 4)
        remote(c3_src, c3_buf.at[spot], p4_s.at[k], p4_r.at[spot], (to, y)).wait_send()


def exchange(packed, proj, coup, far, n_gx, n_gy):
    rows, panels = packed.shape
    rhs = proj.shape[1] // 2
    vmem = pl.BlockSpec(memory_space=pltpu.VMEM)
    f32 = jnp.float32
    sems = pltpu.SemaphoreType.DMA
    return pl.pallas_call(
        functools.partial(exchange_kernel, n_gx, n_gy),
        out_shape=(
            jax.ShapeDtypeStruct((9, rows, panels), jnp.bfloat16),
            jax.ShapeDtypeStruct((128, rhs), jnp.bfloat16),
        ),
        in_specs=[vmem, vmem, vmem, pl.BlockSpec(memory_space=pltpu.SMEM)],
        out_specs=(vmem, vmem),
        scratch_shapes=[
            pltpu.VMEM((n_gy, 64, 2 * rhs), f32),
            pltpu.VMEM((48, 2 * rhs), f32),
            pltpu.VMEM((n_gx, 48, 2 * rhs), f32),
            pltpu.VMEM((n_gx // 4, 32, rhs), f32),
            pltpu.VMEM((512, rhs), f32),
            pltpu.VMEM((48, 2 * rhs), f32),
            pltpu.VMEM((n_gy, 48, 2 * rhs), f32),
            pltpu.VMEM((16, 2 * rhs), f32),
            pltpu.VMEM((4, 16, 2 * rhs), f32),
            sems((9,)), sems((9,)),
            sems((n_gy,)), sems((n_gy,)),
            sems((n_gx,)), sems((n_gx,)),
            sems((n_gy,)), sems((n_gy,)),
            sems((4,)), sems((4,)),
        ],
        compiler_params=pltpu.CompilerParams(
            collective_id=0, has_side_effects=True, vmem_limit_bytes=32 * 1024 * 1024
        ),
    )(packed, proj, coup, far)


def near_kernel(slots, leaf_dev, index, shift, count, live, halo, tfeat, out, sfeat):
    leaf = pl.program_id(0)
    rhs = out.shape[1]

    @pl.when(leaf == 0)
    def _():
        def source_features(place, carry):
            def row(c):
                wide = halo[place, pl.ds(leaf_dev * rhs, 4 * leaf_dev), :].astype(jnp.float32)
                return wide[c * leaf_dev : (c + 1) * leaf_dev]

            sx, sy, sz, area = row(0), row(1), row(2), row(3)
            dx = (place // 3 - 1).astype(jnp.float32)
            dy = (lax.rem(place, 3) - 1).astype(jnp.float32)
            sx, sy = sx + dx, sy + dy
            factor = FOUR_PI / area
            factor = factor * factor

            def split(v):
                high = v.astype(jnp.bfloat16).astype(jnp.float32)
                mid = (v - high).astype(jnp.bfloat16).astype(jnp.float32)
                return [high, mid, v - high - mid]

            high, mid, low = split(factor)
            along_z = split(factor * sz)
            rows = split(factor * sx) + split(factor * sy) + along_z + along_z
            rows += [high, high, high, mid, mid, low]
            rows += split(factor * (sx * sx + sy * sy + sz * sz + area))
            rows += [jnp.zeros_like(factor)] * (24 - len(rows))
            own = pl.ds(pl.multiple_of(place * leaf_dev, leaf_dev), leaf_dev)
            sfeat[own, 24:, :] = jnp.zeros((leaf_dev, FEATURES - 24, halo.shape[2]), jnp.float32)
            for k, value in enumerate(rows):
                sfeat[own, k, :] = value
            return carry

        lax.fori_loop(0, 9, source_features, 0)

    out[0] = jnp.zeros(out.shape[1:], jnp.float32)

    def step(pair, carry):
        total = None
        for u in range(UNROLL):
            at = leaf * slots + pair * UNROLL + u
            n = index[at]
            squared = lax.dot_general(
                sfeat[n].astype(jnp.bfloat16), tfeat[0, shift[at]], (((0,), (0,)), ((), ())),
                preferred_element_type=jnp.float32,
            )
            kernel = lax.rsqrt(squared).astype(jnp.bfloat16)
            src = halo[n // 8, pl.ds(pl.multiple_of(lax.rem(n, 8) * rhs, rhs), rhs), :]
            term = lax.dot_general(
                src * live[at].astype(jnp.bfloat16), kernel, (((1,), (0,)), ((), ())),
                preferred_element_type=jnp.float32,
            )
            total = term if total is None else total + term
        out[0] += total
        return carry

    lax.fori_loop(0, (count[leaf] + UNROLL - 1) // UNROLL, step, 0)


def pieces(v):
    high = lax.reduce_precision(v, 8, 7)
    rest = v - high
    mid = lax.reduce_precision(rest, 8, 7)
    return [high, mid, lax.reduce_precision(rest - mid, 8, 7)]


def near(halo, tfeat, index, shift, count, live, leaf_dev, rhs, slots):
    panels = halo.shape[2]
    whole = lambda *shape: pl.BlockSpec(shape, lambda l, *_: (0,) * len(shape))
    return pl.pallas_call(
        functools.partial(near_kernel, slots, leaf_dev),
        out_shape=jax.ShapeDtypeStruct((leaf_dev, rhs, panels), jnp.float32),
        grid_spec=pltpu.PrefetchScalarGridSpec(
            num_scalar_prefetch=4,
            grid=(leaf_dev,),
            in_specs=[
                whole(*halo.shape),
                pl.BlockSpec((1, 3, FEATURES, panels), lambda l, *_: (l, 0, 0, 0)),
            ],
            out_specs=pl.BlockSpec((1, rhs, panels), lambda l, *_: (l, 0, 0)),
            scratch_shapes=[
                pltpu.VMEM((9 * leaf_dev, FEATURES, panels), jnp.float32),
            ],
        ),
        compiler_params=pltpu.CompilerParams(vmem_limit_bytes=32 * 1024 * 1024),
    )(index, shift, count, live, halo, tfeat)


def body(sources, geometry, near_lists, far_lists, bases_in, bases_out, couplings):
    leaf_dev, rhs, panels = sources.shape[2:]
    slots = near_lists.shape[3]
    n_gx, n_gy = lax.axis_size("gx"), lax.axis_size("gy")
    row_pos, col_pos = lax.axis_index("gx"), lax.axis_index("gy")
    geo = geometry[0, 0]
    by_row = jnp.transpose(geo, (1, 0, 2)).reshape(4 * leaf_dev, panels)
    packed = jnp.concatenate([sources.reshape(leaf_dev * rhs, panels), by_row], axis=0)
    projection = jnp.einsum(
        "aqlp,lrp->aqr", bases_in[0, 0], sources[0, 0], preferred_element_type=jnp.float32
    )
    level_pairs = projection.reshape(2, 64, rhs)
    halo, target = exchange(
        packed, jnp.concatenate([level_pairs[0], level_pairs[1]], axis=1), couplings[0, 0], far_lists[0, 0], n_gx, n_gy
    )

    lists = near_lists[0, 0]
    live = lists >= 0
    own_leaf = jnp.arange(leaf_dev, dtype=jnp.int32)
    device = lists // leaf_dev
    src_leaf = lists % leaf_dev
    local = ((device // n_gy - row_pos + 1) * 3 + device % n_gy - col_pos + 1) * leaf_dev + src_leaf
    index = jnp.where(live, local, 4 * leaf_dev + own_leaf[:, None])
    shift = jnp.where(live, src_leaf - own_leaf[:, None] + 1, 1)
    count = jnp.sum(live.astype(jnp.int32), axis=1)

    t = geo.astype(jnp.float32)[:, None]
    tx, ty, tz = t[:, :, 0], t[:, :, 1], t[:, :, 2]
    dz = jnp.arange(-1, 2, dtype=jnp.float32)[None, :, None]
    shape = (leaf_dev, 3, panels)
    full = lambda v: jnp.broadcast_to(v, shape)
    one, zero = jnp.ones(shape, jnp.float32), jnp.zeros(shape, jnp.float32)
    p = tx * tx + ty * ty + (tz - dz) * (tz - dz)
    high, mid, low = pieces(p)
    rows = [full(-2 * tx)] * 3 + [full(-2 * ty)] * 3 + [full(-2 * tz)] * 3 + [full(2 * dz)] * 3
    rows += [high, mid, low, high, mid, high] + [one] * 3
    rows += [zero] * (FEATURES - len(rows))
    tfeat = jnp.stack(rows, axis=2).astype(jnp.bfloat16)

    near_field = near(
        halo, tfeat,
        index.reshape(-1), shift.reshape(-1), count, live.astype(jnp.int32).reshape(-1),
        leaf_dev, rhs, slots,
    )
    far_field = jnp.einsum(
        "aqr,aqlp->lrp", target.reshape(4, 32, rhs), bases_out[0, 0],
        preferred_element_type=jnp.float32,
    )
    return (near_field + far_field).reshape(sources.shape)


def solution(mesh):
    in_specs = (
        P("gx", "gy", None, None, None),
        P("gx", "gy", None, None, None),
        P("gx", "gy", None, None),
        P("gx", "gy", None, None),
        P("gx", "gy", None, None, None, None),
        P("gx", "gy", None, None, None, None),
        P("gx", "gy", None, None, None),
    )
    out_specs = P("gx", "gy", None, None, None)
    return jax.shard_map(body, mesh=mesh, in_specs=in_specs, out_specs=out_specs, check_vma=False)
```
